256 devices in a mesh: rep: 4 (over y), fsdp: 64 (over x, z, core).
Axes of the slice: x: 4, y: 4, z: 8, core: 2. Of those that a mesh axis runs over, the one named last changes fastest.
Arguments:
- gradients: bfloat16 [4, 256, 512, 512], P('rep', None, 'fsdp'), may hold values from -0.3125 to 0.3125
- block_owners: int32 [256, 1], replicated, may hold values from 0 to 63; in each aligned block of 64 rows (0 to 63, 64 to 127, ...) at most 2 rows name the same one
- left_stats: float32 [512, 512, 512], P(('rep', 'fsdp')), as said below
- right_stats: float32 [512, 512, 512], P(('rep', 'fsdp')), as said below
- left_roots: bfloat16 [512, 512, 512], P(('rep', 'fsdp')), as said below
- right_roots: bfloat16 [512, 512, 512], P(('rep', 'fsdp')), as said below
Outputs:
- update: bfloat16 [256, 512, 512], P('rep', 'fsdp')
- left_new: float32 [512, 512, 512], P(('rep', 'fsdp'))
- right_new: float32 [512, 512, 512], P(('rep', 'fsdp'))
The draws below stay inside these ranges and needn't reach their ends.
Inputs may be any that keep to these rules, and one draw needn't show every extreme that they name: `block_owners`: within each quarter of 64 consecutive blocks no owner appears more than 2 times, and in some quarter some owner appears exactly 2 times. `left_stats`: symmetric blocks with a positive diagonal. `right_stats`: symmetric blocks with a positive diagonal. `left_roots`: symmetric blocks with a positive diagonal. `right_roots`: symmetric blocks with a positive diagonal.
All inputs are finite; a program needn't handle non-finite values.
Results may differ from the reference program's by a relative error of at most 0.018.
Values may be sent and summed in bfloat16 or wider, within the bound.
No kernel may reach another device: no remote copies, remote signals or barrier semaphores. Data moves between devices by JAX's collectives and lax.ppermute only.
A program may use at most 64 MiB of HBM per device.

```python
import math
import jax
import jax.numpy as jnp
import numpy as np
from jax import lax

BLOCK = 512
SLOTS = 2
BLOCKS_REP = 64
NBLOCKS = 256
STAT_SLOTS = 512
N_REP = 4
N_FSDP = 64


def dominant_blocks(key, lowest, highest, off_scale):
    key_diag, key_off = jax.random.split(key)
    diagonal = jax.random.uniform(key_diag, (STAT_SLOTS, BLOCK), jnp.float32, lowest, highest)
    normals = jax.random.normal(key_off, (STAT_SLOTS, BLOCK, BLOCK), jnp.float32)
    symmetric = (normals + jnp.swapaxes(normals, 1, 2)) * (off_scale * 0.70710678)
    on_diagonal = lax.broadcasted_iota(jnp.int32, (BLOCK, BLOCK), 0) == lax.broadcasted_iota(jnp.int32, (BLOCK, BLOCK), 1)
    return jnp.where(on_diagonal[None], diagonal[:, :, None], symmetric)


def draw_left_stats(key, part):
    key = jax.random.fold_in(key, 11)
    return dominant_blocks(key, 0.5, 2.0, 0.05)


def draw_right_stats(key, part):
    key = jax.random.fold_in(key, 23)
    return dominant_blocks(key, 0.5, 2.0, 0.05)


def draw_left_roots(key, part):
    key = jax.random.fold_in(key, 37)
    return dominant_blocks(key, 2.0, 6.0, 2.0 / math.sqrt(BLOCK)).astype(jnp.bfloat16)


def draw_right_roots(key, part):
    key = jax.random.fold_in(key, 41)
    return dominant_blocks(key, 2.0, 6.0, 2.0 / math.sqrt(BLOCK)).astype(jnp.bfloat16)


def shard_levels(own_key, shape, pieces, smallest, high):
    gain, own = 1.0, jax.random.fold_in(own_key, 6)
    for dim, blocks in pieces:
        steps = jnp.exp(jax.random.uniform(jax.random.fold_in(own, dim), (blocks,), jnp.float32, smallest / len(pieces), high / len(pieces)))
        gain = gain * jnp.repeat(steps, shape[dim] // blocks).reshape([-1 if axis == dim else 1 for axis in range(len(shape))])
    return gain


def routed_block(stream_key, own, number, rows, count, top, reach, skew):
    order = jax.random.permutation(stream_key, count)
    packed, common = load_shares(count, rows * top, reach, skew, True), load_shares(count, rows * top, reach, skew, False)
    places = jnp.arange(count)

    def named(sizes, turn):
        used = int((sizes > 0).sum())
        fixed = max(1, used // 4)
        moved = fixed + (places - fixed + turn * (used - fixed)) % max(1, count - fixed)
        return jnp.zeros((count,), jnp.int32).at[order[jnp.where(places < fixed, places, moved)]].set(jnp.asarray(sizes, jnp.int32))

    sizes = jnp.where(number % 4 == 0, named(packed, number // 4), named(common, number - number // 4 - 1))
    mixed = jax.random.permutation(jax.random.fold_in(own, 3), count)
    source_of, receiver = mixed[0:count // 2 * 2:2], mixed[1:count // 2 * 2:2]
    margin = jnp.minimum(sizes[source_of] - 1, reach - sizes[receiver]) // 2
    margin = jnp.where((source_of == order[0]) | (receiver == order[0]) | (sizes[receiver] == 0), 0, jnp.maximum(margin, 0))
    moved = jax.random.randint(jax.random.fold_in(own, 4), (count // 2,), 0, 1 << 20) % (margin + 1)
    sizes = sizes.at[source_of].add(-moved).at[receiver].add(moved)
    labels = jnp.searchsorted(jnp.cumsum(sizes), jnp.arange(rows * top), side="right").astype(jnp.int32)
    grid = labels.reshape(top, rows).T
    grid = grid[jax.random.permutation(jax.random.fold_in(own, 1), rows)]
    turn = jax.random.randint(jax.random.fold_in(own, 2), (rows, 1), 0, top)
    return jnp.take_along_axis(grid, (jnp.arange(top)[None, :] + turn) % top, axis=1)


def load_shares(number_of, total, reach, skew, full):
    portions = [(1 << 20) // math.isqrt(grade ** skew) + 1 for grade in range(1, number_of + 1)]
    largest = reach if full else min(reach, max(-(-total // number_of), total * portions[0] // sum(portions)))
    least = 1 if total - largest >= number_of - 1 else 0
    given, spare = [largest] + [least] * (number_of - 1), total - largest - least * (number_of - 1)
    while spare > 0:
        candidates = [i for i in range(1, number_of) if given[i] < largest] or [i for i in range(1, number_of) if given[i] < reach]
        whole, remaining = sum([portions[i] for i in candidates]), spare
        for i in candidates:
            extra = min(reach - given[i], max(1, remaining * portions[i] // whole), spare)
            given[i] = given[i] + extra
            spare = spare - extra
    return np.array(given)


def normal_values(own_key, shape, width, most, shards=(), held_as=jnp.bfloat16):
    result = width * jax.random.normal(own_key, shape, jnp.float32)
    if shards:
        result = result * shard_levels(own_key, shape, shards, -0.22, 0.18)
    return jnp.clip(result, -most, most).astype(held_as)


def setup_inputs(seed: int = 0) -> dict:
    keys = jax.random.split(jax.random.key(seed), 7)
    gradients = normal_values(keys[0], (N_REP, NBLOCKS, BLOCK, BLOCK), 0.022, 0.3125, ((0, 4), (2, 64)))
    block_owners_keys = jax.random.split(jax.random.fold_in(keys[1], 1), NBLOCKS // BLOCKS_REP)
    block_owners_turns = jax.random.permutation(jax.random.fold_in(keys[1], 3), NBLOCKS // BLOCKS_REP)
    block_owners = jax.vmap(lambda own, number: routed_block(jax.random.fold_in(keys[1], 2), own, number, BLOCKS_REP, N_FSDP, 1, SLOTS, 2))(block_owners_keys, block_owners_turns).reshape((NBLOCKS, 1))
    left_stats = draw_left_stats(jax.random.fold_in(keys[6], 71), 0)
    right_stats = draw_right_stats(jax.random.fold_in(keys[6], 71), 0)
    left_roots = draw_left_roots(jax.random.fold_in(keys[6], 71), 0)
    right_roots = draw_right_roots(jax.random.fold_in(keys[6], 71), 0)
    return dict(gradients=gradients, block_owners=block_owners, left_stats=left_stats, right_stats=right_stats, left_roots=left_roots, right_roots=right_roots)


def reference(gradients, block_owners, left_stats, right_stats, left_roots, right_roots):
    summed = jnp.sum(gradients.astype(jnp.float32), axis=0)
    owner_table = block_owners[:, 0].astype(jnp.int32).reshape(N_REP, BLOCKS_REP)
    same_owner = owner_table[:, :, None] == owner_table[:, None, :]
    position = jnp.arange(BLOCKS_REP, dtype=jnp.int32)
    earlier = position[None, :] < position[:, None]
    slot_rank = jnp.sum((same_owner & earlier[None]).astype(jnp.int32), axis=2).astype(jnp.int32)
    quarter = jnp.arange(N_REP, dtype=jnp.int32)[:, None]
    slot_index = ((quarter * N_FSDP + owner_table) * SLOTS + slot_rank).reshape(NBLOCKS).astype(jnp.int32)
    blocks = jnp.zeros((STAT_SLOTS, BLOCK, BLOCK), jnp.float32).at[slot_index].set(summed)
    left_new = left_stats + jnp.einsum("sij,skj->sik", blocks, blocks, precision=lax.Precision.HIGHEST)
    right_new = right_stats + jnp.einsum("sji,sjk->sik", blocks, blocks, precision=lax.Precision.HIGHEST)
    rounded = blocks.astype(jnp.bfloat16)
    left_half = jnp.einsum("sij,sjk->sik", left_roots.astype(jnp.float32), rounded.astype(jnp.float32)).astype(jnp.bfloat16)
    update_slots = jnp.einsum("sij,sjk->sik", left_half.astype(jnp.float32), right_roots.astype(jnp.float32)).astype(jnp.bfloat16)
    update = update_slots[slot_index]
    return update, left_new, right_new
```

```python
import jax
import jax.numpy as jnp
from jax import lax
from jax.experimental import pallas as pl
from jax.experimental.pallas import tpu as pltpu
from jax.sharding import PartitionSpec as P

MIB = 1024 * 1024
IN_VMEM = pl.BlockSpec(memory_space=pltpu.VMEM)
IN_SMEM = pl.BlockSpec(memory_space=pltpu.SMEM)
ANYWHERE = pl.BlockSpec(memory_space=pl.ANY)


def my_table(block_owners, quarter, per_quarter):
    owners = lax.dynamic_slice(block_owners, (quarter * per_quarter, 0), (per_quarter, 1))
    same_owner = owners == owners.reshape(1, per_quarter)
    earlier = lax.broadcasted_iota(jnp.int32, (per_quarter, per_quarter), 1) < lax.broadcasted_iota(
        jnp.int32, (per_quarter, per_quarter), 0
    )
    rank = jnp.sum((same_owner & earlier).astype(jnp.int32), axis=1)
    return owners[:, 0], rank


def wide(value):
    return value.astype(jnp.float32)


def cut_kernel(starts_ref, rows_ref, *refs):
    outs, sems = refs[:-1], refs[-1]
    copies = []
    for i, out in enumerate(outs):
        copies.append(
            pltpu.make_async_copy(rows_ref.at[pl.ds(starts_ref[i], out.shape[0])], out, sems.at[i])
        )
    for copy in copies:
        copy.start()
    for copy in copies:
        copy.wait()


def cut(rows, starts, counts):
    return pl.pallas_call(
        cut_kernel,
        in_specs=[IN_SMEM, ANYWHERE],
        out_specs=[IN_VMEM] * len(counts),
        out_shape=[jax.ShapeDtypeStruct((count,) + rows.shape[1:], rows.dtype) for count in counts],
        scratch_shapes=[pltpu.SemaphoreType.DMA((len(counts),))],
        compiler_params=pltpu.CompilerParams(vmem_limit_bytes=8 * MIB),
        cost_estimate=pl.CostEstimate(flops=0, bytes_accessed=2 * MIB, transcendentals=0),
    )(jnp.stack(starts), rows)


def add_kernel(a_ref, b_ref, c_ref, d_ref, ab_ref, cd_ref):
    ab_ref[...] = (wide(a_ref[...]) + wide(b_ref[...])).astype(jnp.bfloat16)
    cd_ref[...] = (wide(c_ref[...]) + wide(d_ref[...])).astype(jnp.bfloat16)


def add_pairs(a, b, c, d):
    return pl.pallas_call(
        add_kernel,
        in_specs=[IN_VMEM] * 4,
        out_specs=[IN_VMEM] * 2,
        out_shape=[jax.ShapeDtypeStruct(a.shape, a.dtype)] * 2,
        compiler_params=pltpu.CompilerParams(vmem_limit_bytes=8 * MIB),
        cost_estimate=pl.CostEstimate(flops=2 * a.size, bytes_accessed=2 * MIB, transcendentals=0),
    )(a, b, c, d)


def place_kernel(owner_ref, rank_ref, own_ref, near_a_ref, near_b_ref, far_a_ref, far_b_ref, out_ref):
    out_ref[...] = jnp.zeros_like(out_ref)
    half = near_a_ref.shape[0]

    def step(i, carry):
        for k, near, far in ((i, near_a_ref, far_a_ref), (i + half, near_b_ref, far_b_ref)):
            total = wide(own_ref[k]) + wide(near[i]) + wide(far[i])
            out_ref[owner_ref[k], rank_ref[k]] = total.astype(jnp.bfloat16)
        return carry

    lax.fori_loop(0, half, step, 0, unroll=4)


def place(owners, rank, own, near_a, near_b, far_a, far_b, owner_count, slot_count):
    shape = (owner_count, slot_count) + own.shape[1:]
    return pl.pallas_call(
        place_kernel,
        in_specs=[IN_SMEM] * 2 + [IN_VMEM] * 5,
        out_specs=IN_VMEM,
        out_shape=jax.ShapeDtypeStruct(shape, jnp.bfloat16),
        compiler_params=pltpu.CompilerParams(vmem_limit_bytes=8 * MIB),
        cost_estimate=pl.CostEstimate(flops=2 * own.size, bytes_accessed=3 * MIB, transcendentals=0),
    )(owners, rank, own, near_a, near_b, far_a, far_b)


def product_kernel(held_ref, left_ref, right_ref, update_ref):
    owner_count, slot_count, rows, order = held_ref.shape
    for s in range(slot_count):
        block = wide(held_ref[:, s]).reshape(order, order).astype(jnp.bfloat16)
        half = jnp.dot(left_ref[s], block, preferred_element_type=jnp.float32).astype(jnp.bfloat16)
        full = jnp.dot(half, right_ref[s], preferred_element_type=jnp.float32)
        update_ref[:, s] = full.reshape(owner_count, rows, order).astype(jnp.bfloat16)


def products(held, left_roots, right_roots):
    return pl.pallas_call(
        product_kernel,
        in_specs=[IN_VMEM] * 3,
        out_specs=IN_VMEM,
        out_shape=jax.ShapeDtypeStruct(held.shape, jnp.bfloat16),
        compiler_params=pltpu.CompilerParams(vmem_limit_bytes=16 * MIB),
        cost_estimate=pl.CostEstimate(flops=2**30, bytes_accessed=4 * MIB, transcendentals=0),
    )(held, left_roots, right_roots)


def stats_kernel(held_ref, left_ref, right_ref, left_out, right_out):
    order = held_ref.shape[3]
    block = wide(held_ref[:, 0]).reshape(order, order).astype(jnp.bfloat16)
    left_out[0] = left_ref[0] + lax.dot_general(
        block, block, (((1,), (1,)), ((), ())), preferred_element_type=jnp.float32
    )
    right_out[0] = right_ref[0] + lax.dot_general(
        block, block, (((0,), (0,)), ((), ())), preferred_element_type=jnp.float32
    )


def statistics(held, left_stats, right_stats):
    owner_count, slot_count, rows, order = held.shape
    matrix = pl.BlockSpec((1, order, order), lambda s: (s, 0, 0))
    return pl.pallas_call(
        stats_kernel,
        grid=(slot_count,),
        in_specs=[pl.BlockSpec((owner_count, 1, rows, order), lambda s: (0, s, 0, 0)), matrix, matrix],
        out_specs=[matrix] * 2,
        out_shape=[jax.ShapeDtypeStruct(left_stats.shape, jnp.float32)] * 2,
        compiler_params=pltpu.CompilerParams(vmem_limit_bytes=24 * MIB),
        cost_estimate=pl.CostEstimate(flops=2**30, bytes_accessed=10 * MIB, transcendentals=0),
    )(held, left_stats, right_stats)


def take_kernel(owner_ref, rank_ref, held_ref, out_ref, gathered, sems):
    count = gathered.shape[0]
    parts = sems.shape[0]
    size = count // parts
    copies = []
    for part in range(parts):
        def step(i, carry):
            k = part * size + i
            gathered[k] = held_ref[owner_ref[k], rank_ref[k]]
            return carry

        lax.fori_loop(0, size, step, 0, unroll=8)
        run = pl.ds(part * size, size)
        copies.append(pltpu.make_async_copy(gathered.at[run], out_ref.at[run], sems.at[part]))
        copies[-1].start()
    for copy in copies:
        copy.wait()


def take(owners, rank, held):
    shape = (owners.shape[0],) + held.shape[2:]
    return pl.pallas_call(
        take_kernel,
        in_specs=[IN_SMEM] * 2 + [IN_VMEM],
        out_specs=ANYWHERE,
        out_shape=jax.ShapeDtypeStruct(shape, jnp.bfloat16),
        scratch_shapes=[pltpu.VMEM(shape, jnp.bfloat16), pltpu.SemaphoreType.DMA((4,))],
        compiler_params=pltpu.CompilerParams(vmem_limit_bytes=8 * MIB),
        cost_estimate=pl.CostEstimate(flops=0, bytes_accessed=2 * MIB, transcendentals=0),
    )(owners, rank, held)


def on_device(gradients, block_owners, left_stats, right_stats, left_roots, right_roots):
    rep_count = lax.axis_size("rep")
    owner_count = lax.axis_size("fsdp")
    slot_count = left_stats.shape[0]
    replica_rows = gradients[0]
    per_quarter = replica_rows.shape[0] // rep_count
    half = per_quarter // 2
    quarter = lax.axis_index("rep")

    def swap(value, bit):
        return lax.ppermute(value, "rep", [(i, i ^ bit) for i in range(rep_count)])

    def start(bit, second):
        return (quarter ^ bit) * per_quarter + second * half

    on_a, on_b, end_a, end_b = cut(
        replica_rows, [start(2, 0), start(2, 1), start(1, 0), start(3, 1)], [half] * 4
    )
    on_a, on_b = swap(on_a, 1), swap(on_b, 3)
    near_a, near_b = swap(end_a, 1), swap(end_b, 3)
    own, pass_a, pass_b = cut(
        replica_rows, [start(0, 0), start(3, 0), start(1, 1)], [per_quarter, half, half]
    )
    on_a, on_b = add_pairs(pass_a, on_a, pass_b, on_b)
    far_a, far_b = swap(on_a, 3), swap(on_b, 1)

    owners, rank = my_table(block_owners, quarter, per_quarter)
    placed = place(owners, rank, own, near_a, near_b, far_a, far_b, owner_count, slot_count)
    held = lax.all_to_all(placed, "fsdp", split_axis=0, concat_axis=0, tiled=True)
    update_slots = products(held, left_roots, right_roots)
    returned = lax.all_to_all(update_slots, "fsdp", split_axis=0, concat_axis=0, tiled=True)
    left_new, right_new = statistics(held, left_stats, right_stats)
    update = take(owners, rank, returned)
    return (update, left_new, right_new)


def solution(mesh):
    placed = (
        P("rep", None, "fsdp", None),
        P(),
        P(("rep", "fsdp"), None, None),
        P(("rep", "fsdp"), None, None),
        P(("rep", "fsdp"), None, None),
        P(("rep", "fsdp"), None, None),
    )
    return jax.shard_map(
        on_device,
        mesh=mesh,
        in_specs=placed,
        out_specs=(
            P("rep", "fsdp", None),
            P(("rep", "fsdp"), None, None),
            P(("rep", "fsdp"), None, None),
        ),
        check_vma=False,
    )
```

```python
import jax
import jax.numpy as jnp
from jax import lax
from jax.experimental import pallas as pl
from jax.experimental.pallas import tpu as pltpu
from jax.sharding import PartitionSpec as P

MIB = 1024 * 1024
IN_VMEM = pl.BlockSpec(memory_space=pltpu.VMEM)
IN_SMEM = pl.BlockSpec(memory_space=pltpu.SMEM)
ANYWHERE = pl.BlockSpec(memory_space=pl.ANY)
IN_HBM = pl.BlockSpec(memory_space=pltpu.HBM)


def my_table(block_owners, quarter, per_quarter):
    owners = lax.dynamic_slice(block_owners, (quarter * per_quarter, 0), (per_quarter, 1))
    same_owner = owners == owners.reshape(1, per_quarter)
    earlier = lax.broadcasted_iota(jnp.int32, (per_quarter, per_quarter), 1) < lax.broadcasted_iota(
        jnp.int32, (per_quarter, per_quarter), 0
    )
    rank = jnp.sum((same_owner & earlier).astype(jnp.int32), axis=1)
    return owners[:, 0], rank


def wide(value):
    return value.astype(jnp.float32)


def cut_kernel(starts_ref, rows_ref, *refs):
    outs, sems = refs[:-1], refs[-1]
    copies = []
    for i, out in enumerate(outs):
        copies.append(
            pltpu.make_async_copy(rows_ref.at[pl.ds(starts_ref[i], out.shape[0])], out, sems.at[i])
        )
    for copy in copies:
        copy.start()
    for copy in copies:
        copy.wait()


def cut(rows, starts, counts):
    return pl.pallas_call(
        cut_kernel,
        in_specs=[IN_SMEM, IN_HBM],
        out_specs=[IN_VMEM] * len(counts),
        out_shape=[pltpu.VMEM((count,) + rows.shape[1:], rows.dtype) for count in counts],
        scratch_shapes=[pltpu.SemaphoreType.DMA((len(counts),))],
        compiler_params=pltpu.CompilerParams(vmem_limit_bytes=8 * MIB),
        cost_estimate=pl.CostEstimate(flops=0, bytes_accessed=2 * MIB, transcendentals=0),
    )(jnp.stack(starts), pltpu.with_memory_space_constraint(rows, pltpu.HBM))


def add_kernel(a_ref, b_ref, sum_ref):
    sum_ref[...] = (wide(a_ref[...]) + wide(b_ref[...])).astype(jnp.bfloat16)


def add(a, b):
    return pl.pallas_call(
        add_kernel,
        in_specs=[IN_VMEM] * 2,
        out_specs=IN_VMEM,
        out_shape=jax.ShapeDtypeStruct(a.shape, a.dtype),
        compiler_params=pltpu.CompilerParams(vmem_limit_bytes=8 * MIB),
        cost_estimate=pl.CostEstimate(flops=a.size, bytes_accessed=MIB, transcendentals=0),
    )(a, b)


def place_kernel(owner_ref, rank_ref, own_ref, near_a_ref, near_b_ref, far_a_ref, far_b_ref, out_ref):
    out_ref[...] = jnp.zeros_like(out_ref)
    half = near_a_ref.shape[0]

    def step(i, carry):
        for k, near, far in ((i, near_a_ref, far_a_ref), (i + half, near_b_ref, far_b_ref)):
            total = wide(own_ref[k]) + wide(near[i]) + wide(far[i])
            out_ref[owner_ref[k], rank_ref[k]] = total.astype(jnp.bfloat16)
        return carry

    lax.fori_loop(0, half, step, 0, unroll=4)


def place(owners, rank, own, near_a, near_b, far_a, far_b, owner_count, slot_count):
    shape = (owner_count, slot_count) + own.shape[1:]
    return pl.pallas_call(
        place_kernel,
        in_specs=[IN_SMEM] * 2 + [IN_VMEM] * 5,
        out_specs=IN_VMEM,
        out_shape=jax.ShapeDtypeStruct(shape, jnp.bfloat16),
        compiler_params=pltpu.CompilerParams(vmem_limit_bytes=8 * MIB),
        cost_estimate=pl.CostEstimate(flops=2 * own.size, bytes_accessed=3 * MIB, transcendentals=0),
    )(owners, rank, own, near_a, near_b, far_a, far_b)


def product_kernel(held_ref, left_ref, right_ref, update_ref, made, sems):
    owner_count, slot_count, rows, order = held_ref.shape
    strips = sems.shape[1]
    height = order // strips
    copies = []
    for s in range(slot_count):
        block = wide(held_ref[:, s]).reshape(order, order).astype(jnp.bfloat16)
        half = jnp.dot(left_ref[s], block, preferred_element_type=jnp.float32).astype(jnp.bfloat16)
        for j in range(strips):
            full = jnp.dot(
                half[j * height : (j + 1) * height], right_ref[s], preferred_element_type=jnp.float32
            )
            run = pl.ds(j * height // rows, height // rows)
            made[s, run] = full.reshape(height // rows, rows, order).astype(jnp.bfloat16)
            copies.append(pltpu.make_async_copy(made.at[s, run], update_ref.at[run, s], sems.at[s, j]))
            copies[-1].start()
    for copy in copies:
        copy.wait()


def products(held, left_roots, right_roots):
    owner_count, slot_count, rows, order = held.shape
    return pl.pallas_call(
        product_kernel,
        in_specs=[IN_VMEM] * 3,
        out_specs=ANYWHERE,
        out_shape=jax.ShapeDtypeStruct(held.shape, jnp.bfloat16),
        scratch_shapes=[
            pltpu.VMEM((slot_count, owner_count, rows, order), jnp.bfloat16),
            pltpu.SemaphoreType.DMA((slot_count, 2)),
        ],
        compiler_params=pltpu.CompilerParams(vmem_limit_bytes=16 * MIB),
        cost_estimate=pl.CostEstimate(flops=2**30, bytes_accessed=4 * MIB, transcendentals=0),
    )(held, left_roots, right_roots)


def stats_kernel(held_ref, left_ref, right_ref, left_out, right_out):
    order = held_ref.shape[3]
    block = wide(held_ref[:, 0]).reshape(order, order).astype(jnp.bfloat16)
    left_out[0] = left_ref[0] + lax.dot_general(
        block, block, (((1,), (1,)), ((), ())), preferred_element_type=jnp.float32
    )
    right_out[0] = right_ref[0] + lax.dot_general(
        block, block, (((0,), (0,)), ((), ())), preferred_element_type=jnp.float32
    )


def statistics(held, left_stats, right_stats):
    owner_count, slot_count, rows, order = held.shape
    matrix = pl.BlockSpec((1, order, order), lambda s: (s, 0, 0))
    return pl.pallas_call(
        stats_kernel,
        grid=(slot_count,),
        in_specs=[pl.BlockSpec((owner_count, 1, rows, order), lambda s: (0, s, 0, 0)), matrix, matrix],
        out_specs=[matrix] * 2,
        out_shape=[jax.ShapeDtypeStruct(left_stats.shape, jnp.float32)] * 2,
        compiler_params=pltpu.CompilerParams(vmem_limit_bytes=24 * MIB),
        cost_estimate=pl.CostEstimate(flops=2**30, bytes_accessed=10 * MIB, transcendentals=0),
    )(held, left_stats, right_stats)


def take_kernel(owner_ref, rank_ref, held_ref, out_ref, gathered, sems):
    count = gathered.shape[0]
    parts = sems.shape[0]
    size = count // parts
    copies = []
    for part in range(parts):
        def step(i, carry):
            k = part * size + i
            gathered[k] = held_ref[owner_ref[k], rank_ref[k]]
            return carry

        lax.fori_loop(0, size, step, 0, unroll=8)
        run = pl.ds(part * size, size)
        copies.append(pltpu.make_async_copy(gathered.at[run], out_ref.at[run], sems.at[part]))
        copies[-1].start()
    for copy in copies:
        copy.wait()


def take(owners, rank, held):
    shape = (owners.shape[0],) + held.shape[2:]
    return pl.pallas_call(
        take_kernel,
        in_specs=[IN_SMEM] * 2 + [IN_VMEM],
        out_specs=ANYWHERE,
        out_shape=jax.ShapeDtypeStruct(shape, jnp.bfloat16),
        scratch_shapes=[pltpu.VMEM(shape, jnp.bfloat16), pltpu.SemaphoreType.DMA((4,))],
        compiler_params=pltpu.CompilerParams(vmem_limit_bytes=8 * MIB),
        cost_estimate=pl.CostEstimate(flops=0, bytes_accessed=2 * MIB, transcendentals=0),
    )(owners, rank, held)


def on_device(gradients, block_owners, left_stats, right_stats, left_roots, right_roots):
    rep_count = lax.axis_size("rep")
    owner_count = lax.axis_size("fsdp")
    slot_count = left_stats.shape[0]
    replica_rows = gradients[0]
    per_quarter = replica_rows.shape[0] // rep_count
    half = per_quarter // 2
    quarter = lax.axis_index("rep")

    def swap(value, bit):
        return lax.ppermute(value, "rep", [(i, i ^ bit) for i in range(rep_count)])

    def start(bit, second):
        return (quarter ^ bit) * per_quarter + second * half

    on_a, on_b = cut(replica_rows, [start(2, 0), start(2, 1)], [half] * 2)
    on_a, on_b = swap(on_a, 1), swap(on_b, 3)
    end_a, end_b = cut(replica_rows, [start(1, 0), start(3, 1)], [half] * 2)
    near_a, near_b = swap(end_a, 1), swap(end_b, 3)
    own, pass_a, pass_b = cut(
        replica_rows, [start(0, 0), start(3, 0), start(1, 1)], [per_quarter, half, half]
    )
    on_a, on_b = add(pass_a, on_a), add(pass_b, on_b)
    far_a, far_b = swap(on_a, 3), swap(on_b, 1)

    owners, rank = my_table(block_owners, quarter, per_quarter)
    placed = place(owners, rank, own, near_a, near_b, far_a, far_b, owner_count, slot_count)
    held = lax.all_to_all(placed, "fsdp", split_axis=0, concat_axis=0, tiled=True)
    update_slots = products(held, left_roots, right_roots)
    returned = lax.all_to_all(update_slots, "fsdp", split_axis=0, concat_axis=0, tiled=True)
    left_new, right_new = statistics(held, left_stats, right_stats)
    update = take(owners, rank, returned)
    return (update, left_new, right_new)


def solution(mesh):
    placed = (
        P("rep", None, "fsdp", None),
        P(),
        P(("rep", "fsdp"), None, None),
        P(("rep", "fsdp"), None, None),
        P(("rep", "fsdp"), None, None),
        P(("rep", "fsdp"), None, None),
    )
    return jax.shard_map(
        on_device,
        mesh=mesh,
        in_specs=placed,
        out_specs=(
            P("rep", "fsdp", None),
            P(("rep", "fsdp"), None, None),
            P(("rep", "fsdp"), None, None),
        ),
        check_vma=False,
    )
```

```python
import jax
import jax.numpy as jnp
from jax import lax
from jax.experimental import pallas as pl
from jax.experimental.pallas import tpu as pltpu
from jax.sharding import PartitionSpec as P

MIB = 1024 * 1024
IN_VMEM = pl.BlockSpec(memory_space=pltpu.VMEM)
IN_SMEM = pl.BlockSpec(memory_space=pltpu.SMEM)
ANYWHERE = pl.BlockSpec(memory_space=pl.ANY)
IN_HBM = pl.BlockSpec(memory_space=pltpu.HBM)


def my_table(block_owners, quarter, per_quarter):
    owners = lax.dynamic_slice(block_owners, (quarter * per_quarter, 0), (per_quarter, 1))
    same_owner = owners == owners.reshape(1, per_quarter)
    earlier = lax.broadcasted_iota(jnp.int32, (per_quarter, per_quarter), 1) < lax.broadcasted_iota(
        jnp.int32, (per_quarter, per_quarter), 0
    )
    rank = jnp.sum((same_owner & earlier).astype(jnp.int32), axis=1)
    return owners[:, 0], rank


def wide(value):
    return value.astype(jnp.float32)


def cut_kernel(starts_ref, rows_ref, *refs):
    outs, sems = refs[:-1], refs[-1]
    copies = []
    for i, out in enumerate(outs):
        copies.append(
            pltpu.make_async_copy(rows_ref.at[pl.ds(starts_ref[i], out.shape[0])], out, sems.at[i])
        )
    for copy in copies:
        copy.start()
    for copy in copies:
        copy.wait()


def cut(rows, starts, counts):
    return pl.pallas_call(
        cut_kernel,
        in_specs=[IN_SMEM, IN_HBM],
        out_specs=[IN_VMEM] * len(counts),
        out_shape=[pltpu.VMEM((count,) + rows.shape[1:], rows.dtype) for count in counts],
        scratch_shapes=[pltpu.SemaphoreType.DMA((len(counts),))],
        compiler_params=pltpu.CompilerParams(vmem_limit_bytes=8 * MIB),
        cost_estimate=pl.CostEstimate(flops=0, bytes_accessed=2 * MIB, transcendentals=0),
    )(jnp.stack(starts), pltpu.with_memory_space_constraint(rows, pltpu.HBM))


def add_kernel(a_ref, b_ref, sum_ref):
    sum_ref[...] = (wide(a_ref[...]) + wide(b_ref[...])).astype(jnp.bfloat16)


def add(a, b):
    return pl.pallas_call(
        add_kernel,
        in_specs=[IN_VMEM] * 2,
        out_specs=IN_VMEM,
        out_shape=jax.ShapeDtypeStruct(a.shape, a.dtype),
        compiler_params=pltpu.CompilerParams(vmem_limit_bytes=8 * MIB),
        cost_estimate=pl.CostEstimate(flops=a.size, bytes_accessed=MIB, transcendentals=0),
    )(a, b)


def near_kernel(own_ref, near_a_ref, near_b_ref, sum_ref):
    half = near_a_ref.shape[0]
    sum_ref[:half] = wide(own_ref[:half]) + wide(near_a_ref[...])
    sum_ref[half:] = wide(own_ref[half:]) + wide(near_b_ref[...])


def near_sum(own, near_a, near_b):
    return pl.pallas_call(
        near_kernel,
        in_specs=[IN_VMEM] * 3,
        out_specs=IN_VMEM,
        out_shape=pltpu.VMEM(own.shape, jnp.float32),
        compiler_params=pltpu.CompilerParams(vmem_limit_bytes=8 * MIB),
        cost_estimate=pl.CostEstimate(flops=own.size, bytes_accessed=2 * MIB, transcendentals=0),
    )(own, near_a, near_b)


def place_kernel(owner_ref, rank_ref, near_ref, far_a_ref, far_b_ref, out_ref):
    out_ref[...] = jnp.zeros_like(out_ref)
    half = far_a_ref.shape[0]

    def step(i, carry):
        for k, far in ((i, far_a_ref), (i + half, far_b_ref)):
            total = near_ref[k] + wide(far[i])
            out_ref[owner_ref[k], rank_ref[k]] = total.astype(jnp.bfloat16)
        return carry

    lax.fori_loop(0, half, step, 0, unroll=8)


def place(owners, rank, near, far_a, far_b, owner_count, slot_count):
    shape = (owner_count, slot_count) + near.shape[1:]
    return pl.pallas_call(
        place_kernel,
        in_specs=[IN_SMEM] * 2 + [IN_VMEM] * 3,
        out_specs=IN_VMEM,
        out_shape=pltpu.VMEM(shape, jnp.bfloat16),
        compiler_params=pltpu.CompilerParams(vmem_limit_bytes=8 * MIB),
        cost_estimate=pl.CostEstimate(flops=near.size, bytes_accessed=3 * MIB, transcendentals=0),
    )(owners, rank, near, far_a, far_b)


def product_kernel(held_ref, left_ref, right_ref, update_ref, made, sems):
    owner_count, slot_count, rows, order = held_ref.shape
    strips = sems.shape[1]
    height = order // strips
    copies = []
    for s in range(slot_count):
        block = wide(held_ref[:, s]).reshape(order, order).astype(jnp.bfloat16)
        half = jnp.dot(left_ref[s], block, preferred_element_type=jnp.float32).astype(jnp.bfloat16)
        for j in range(strips):
            full = jnp.dot(
                half[j * height : (j + 1) * height], right_ref[s], preferred_element_type=jnp.float32
            )
            run = pl.ds(j * height // rows, height // rows)
            made[s, run] = full.reshape(height // rows, rows, order).astype(jnp.bfloat16)
            copies.append(pltpu.make_async_copy(made.at[s, run], update_ref.at[run, s], sems.at[s, j]))
            copies[-1].start()
    for copy in copies:
        copy.wait()


def products(held, left_roots, right_roots):
    owner_count, slot_count, rows, order = held.shape
    return pl.pallas_call(
        product_kernel,
        in_specs=[IN_VMEM] * 3,
        out_specs=ANYWHERE,
        out_shape=jax.ShapeDtypeStruct(held.shape, jnp.bfloat16),
        scratch_shapes=[
            pltpu.VMEM((slot_count, owner_count, rows, order), jnp.bfloat16),
            pltpu.SemaphoreType.DMA((slot_count, 2)),
        ],
        compiler_params=pltpu.CompilerParams(vmem_limit_bytes=16 * MIB),
        cost_estimate=pl.CostEstimate(flops=2**30, bytes_accessed=4 * MIB, transcendentals=0),
    )(held, left_roots, right_roots)


def stats_kernel(held_ref, left_ref, right_ref, left_out, right_out):
    order = held_ref.shape[3]
    block = wide(held_ref[:, 0]).reshape(order, order).astype(jnp.bfloat16)
    left_out[0] = left_ref[0] + lax.dot_general(
        block, block, (((1,), (1,)), ((), ())), preferred_element_type=jnp.float32
    )
    right_out[0] = right_ref[0] + lax.dot_general(
        block, block, (((0,), (0,)), ((), ())), preferred_element_type=jnp.float32
    )


def statistics(held, left_stats, right_stats):
    owner_count, slot_count, rows, order = held.shape
    matrix = pl.BlockSpec((1, order, order), lambda s: (s, 0, 0))
    return pl.pallas_call(
        stats_kernel,
        grid=(slot_count,),
        in_specs=[pl.BlockSpec((owner_count, 1, rows, order), lambda s: (0, s, 0, 0)), matrix, matrix],
        out_specs=[matrix] * 2,
        out_shape=[jax.ShapeDtypeStruct(left_stats.shape, jnp.float32)] * 2,
        compiler_params=pltpu.CompilerParams(vmem_limit_bytes=24 * MIB),
        cost_estimate=pl.CostEstimate(flops=2**30, bytes_accessed=10 * MIB, transcendentals=0),
    )(held, left_stats, right_stats)


def take_kernel(owner_ref, rank_ref, held_ref, out_ref, gathered, sems):
    count = gathered.shape[0]
    parts = sems.shape[0]
    size = count // parts
    copies = []
    for part in range(parts):
        def step(i, carry):
            k = part * size + i
            gathered[k] = held_ref[owner_ref[k], rank_ref[k]]
            return carry

        lax.fori_loop(0, size, step, 0, unroll=8)
        run = pl.ds(part * size, size)
        copies.append(pltpu.make_async_copy(gathered.at[run], out_ref.at[run], sems.at[part]))
        copies[-1].start()
    for copy in copies:
        copy.wait()


def take(owners, rank, held):
    shape = (owners.shape[0],) + held.shape[2:]
    return pl.pallas_call(
        take_kernel,
        in_specs=[IN_SMEM] * 2 + [IN_VMEM],
        out_specs=ANYWHERE,
        out_shape=jax.ShapeDtypeStruct(shape, jnp.bfloat16),
        scratch_shapes=[pltpu.VMEM(shape, jnp.bfloat16), pltpu.SemaphoreType.DMA((4,))],
        compiler_params=pltpu.CompilerParams(vmem_limit_bytes=8 * MIB),
        cost_estimate=pl.CostEstimate(flops=0, bytes_accessed=2 * MIB, transcendentals=0),
    )(owners, rank, held)


def on_device(gradients, block_owners, left_stats, right_stats, left_roots, right_roots):
    rep_count = lax.axis_size("rep")
    owner_count = lax.axis_size("fsdp")
    slot_count = left_stats.shape[0]
    replica_rows = gradients[0]
    per_quarter = replica_rows.shape[0] // rep_count
    half = per_quarter // 2
    quarter = lax.axis_index("rep")

    def swap(value, bit):
        return lax.ppermute(value, "rep", [(i, i ^ bit) for i in range(rep_count)])

    def start(bit, second):
        return (quarter ^ bit) * per_quarter + second * half

    on_a = lax.dynamic_slice_in_dim(replica_rows, start(2, 0), half)
    on_b = lax.dynamic_slice_in_dim(replica_rows, start(2, 1), half)
    on_a, on_b = swap(on_a, 1), swap(on_b, 3)
    end_a, end_b = cut(replica_rows, [start(1, 0), start(3, 1)], [half] * 2)
    near_a, near_b = swap(end_a, 1), swap(end_b, 3)
    own, pass_a, pass_b = cut(
        replica_rows, [start(0, 0), start(3, 0), start(1, 1)], [per_quarter, half, half]
    )
    on_a, on_b = add(pass_a, on_a), add(pass_b, on_b)
    far_a, far_b = swap(on_a, 3), swap(on_b, 1)

    owners, rank = my_table(block_owners, quarter, per_quarter)
    near = near_sum(own, near_a, near_b)
    placed = place(owners, rank, near, far_a, far_b, owner_count, slot_count)
    held = lax.all_to_all(placed, "fsdp", split_axis=0, concat_axis=0, tiled=True)
    update_slots = products(held, left_roots, right_roots)
    returned = lax.all_to_all(update_slots, "fsdp", split_axis=0, concat_axis=0, tiled=True)
    left_new, right_new = statistics(held, left_stats, right_stats)
    update = take(owners, rank, returned)
    return (update, left_new, right_new)


def solution(mesh):
    placed = (
        P("rep", None, "fsdp", None),
        P(),
        P(("rep", "fsdp"), None, None),
        P(("rep", "fsdp"), None, None),
        P(("rep", "fsdp"), None, None),
        P(("rep", "fsdp"), None, None),
    )
    return jax.shard_map(
        on_device,
        mesh=mesh,
        in_specs=placed,
        out_specs=(
            P("rep", "fsdp", None),
            P(("rep", "fsdp"), None, None),
            P(("rep", "fsdp"), None, None),
        ),
        check_vma=False,
    )
```

```python
import jax
import jax.numpy as jnp
from jax import lax
from jax.experimental import pallas as pl
from jax.experimental.pallas import tpu as pltpu
from jax.sharding import PartitionSpec as P

MIB = 1024 * 1024
IN_VMEM = pl.BlockSpec(memory_space=pltpu.VMEM)
IN_SMEM = pl.BlockSpec(memory_space=pltpu.SMEM)
ANYWHERE = pl.BlockSpec(memory_space=pl.ANY)
IN_HBM = pl.BlockSpec(memory_space=pltpu.HBM)


def my_places(block_owners, quarter, per_quarter, slot_count):
    owners = lax.dynamic_slice(block_owners, (quarter * per_quarter, 0), (per_quarter, 1))
    same_owner = owners == owners.reshape(1, per_quarter)
    earlier = lax.broadcasted_iota(jnp.int32, (per_quarter, per_quarter), 1) < lax.broadcasted_iota(
        jnp.int32, (per_quarter, per_quarter), 0
    )
    rank = jnp.sum((same_owner & earlier).astype(jnp.int32), axis=1)
    return owners[:, 0] * slot_count + rank


def wide(value):
    return value.astype(jnp.float32)


def cut_kernel(starts_ref, rows_ref, *refs):
    outs, sems = refs[:-1], refs[-1]
    copies = []
    for i, out in enumerate(outs):
        copies.append(
            pltpu.make_async_copy(rows_ref.at[pl.ds(starts_ref[i], out.shape[0])], out, sems.at[i])
        )
    for copy in copies:
        copy.start()
    for copy in copies:
        copy.wait()


def cut(rows, starts, counts):
    return pl.pallas_call(
        cut_kernel,
        in_specs=[IN_SMEM, IN_HBM],
        out_specs=[IN_VMEM] * len(counts),
        out_shape=[pltpu.VMEM((count,) + rows.shape[1:], rows.dtype) for count in counts],
        scratch_shapes=[pltpu.SemaphoreType.DMA((len(counts),))],
        compiler_params=pltpu.CompilerParams(vmem_limit_bytes=8 * MIB),
        cost_estimate=pl.CostEstimate(flops=0, bytes_accessed=2 * MIB, transcendentals=0),
    )(jnp.stack(starts), pltpu.with_memory_space_constraint(rows, pltpu.HBM))


def add_kernel(a_ref, b_ref, sum_ref):
    sum_ref[...] = (wide(a_ref[...]) + wide(b_ref[...])).astype(jnp.bfloat16)


def add(a, b):
    return pl.pallas_call(
        add_kernel,
        in_specs=[IN_VMEM] * 2,
        out_specs=IN_VMEM,
        out_shape=jax.ShapeDtypeStruct(a.shape, a.dtype),
        compiler_params=pltpu.CompilerParams(vmem_limit_bytes=8 * MIB),
        cost_estimate=pl.CostEstimate(flops=a.size, bytes_accessed=MIB, transcendentals=0),
    )(a, b)


def near_kernel(own_ref, near_a_ref, near_b_ref, sum_ref):
    half = near_a_ref.shape[0]
    sum_ref[:half] = wide(own_ref[:half]) + wide(near_a_ref[...])
    sum_ref[half:] = wide(own_ref[half:]) + wide(near_b_ref[...])


def near_sum(own, near_a, near_b):
    return pl.pallas_call(
        near_kernel,
        in_specs=[IN_VMEM] * 3,
        out_specs=IN_VMEM,
        out_shape=pltpu.VMEM(own.shape, jnp.float32),
        compiler_params=pltpu.CompilerParams(vmem_limit_bytes=8 * MIB),
        cost_estimate=pl.CostEstimate(flops=own.size, bytes_accessed=2 * MIB, transcendentals=0),
    )(own, near_a, near_b)


def place_kernel(place_ref, near_ref, far_a_ref, far_b_ref, out_ref):
    out_ref[...] = jnp.zeros_like(out_ref)
    half = far_a_ref.shape[0]

    def step(i, carry):
        for k, far in ((i, far_a_ref), (i + half, far_b_ref)):
            total = near_ref[k] + wide(far[i])
            out_ref[place_ref[k]] = total.astype(jnp.bfloat16)
        return carry

    lax.fori_loop(0, half, step, 0, unroll=8)


def place(places, near, far_a, far_b, place_count):
    shape = (place_count,) + near.shape[1:]
    return pl.pallas_call(
        place_kernel,
        in_specs=[IN_SMEM] + [IN_VMEM] * 3,
        out_specs=IN_VMEM,
        out_shape=jax.ShapeDtypeStruct(shape, jnp.bfloat16),
        compiler_params=pltpu.CompilerParams(vmem_limit_bytes=8 * MIB),
        cost_estimate=pl.CostEstimate(flops=near.size, bytes_accessed=3 * MIB, transcendentals=0),
    )(places, near, far_a, far_b)


def product_kernel(held_ref, left_ref, right_ref, update_ref, made, sems):
    owner_count, slot_count, rows, order = held_ref.shape
    strips = sems.shape[1]
    height = order // strips
    copies = []
    for s in range(slot_count):
        block = wide(held_ref[:, s]).reshape(order, order).astype(jnp.bfloat16)
        half = jnp.dot(left_ref[s], block, preferred_element_type=jnp.float32).astype(jnp.bfloat16)
        for j in range(strips):
            full = jnp.dot(
                half[j * height : (j + 1) * height], right_ref[s], preferred_element_type=jnp.float32
            )
            run = pl.ds(j * height // rows, height // rows)
            made[s, run] = full.reshape(height // rows, rows, order).astype(jnp.bfloat16)
            copies.append(pltpu.make_async_copy(made.at[s, run], update_ref.at[run, s], sems.at[s, j]))
            copies[-1].start()
    for copy in copies:
        copy.wait()


def products(held, left_roots, right_roots):
    owner_count, slot_count, rows, order = held.shape
    return pl.pallas_call(
        product_kernel,
        in_specs=[IN_VMEM] * 3,
        out_specs=ANYWHERE,
        out_shape=jax.ShapeDtypeStruct(held.shape, jnp.bfloat16),
        scratch_shapes=[
            pltpu.VMEM((slot_count, owner_count, rows, order), jnp.bfloat16),
            pltpu.SemaphoreType.DMA((slot_count, 2)),
        ],
        compiler_params=pltpu.CompilerParams(vmem_limit_bytes=16 * MIB),
        cost_estimate=pl.CostEstimate(flops=2**30, bytes_accessed=4 * MIB, transcendentals=0),
    )(held, left_roots, right_roots)


def stats_kernel(held_ref, left_ref, right_ref, left_out, right_out):
    order = held_ref.shape[3]
    block = wide(held_ref[:, 0]).reshape(order, order).astype(jnp.bfloat16)
    left_out[0] = left_ref[0] + lax.dot_general(
        block, block, (((1,), (1,)), ((), ())), preferred_element_type=jnp.float32
    )
    right_out[0] = right_ref[0] + lax.dot_general(
        block, block, (((0,), (0,)), ((), ())), preferred_element_type=jnp.float32
    )


def statistics(held, left_stats, right_stats):
    owner_count, slot_count, rows, order = held.shape
    matrix = pl.BlockSpec((1, order, order), lambda s: (s, 0, 0))
    return pl.pallas_call(
        stats_kernel,
        grid=(slot_count,),
        in_specs=[pl.BlockSpec((owner_count, 1, rows, order), lambda s: (0, s, 0, 0)), matrix, matrix],
        out_specs=[matrix] * 2,
        out_shape=[jax.ShapeDtypeStruct(left_stats.shape, jnp.float32)] * 2,
        compiler_params=pltpu.CompilerParams(vmem_limit_bytes=24 * MIB),
        cost_estimate=pl.CostEstimate(flops=2**30, bytes_accessed=10 * MIB, transcendentals=0),
    )(held, left_stats, right_stats)


def take_kernel(place_ref, held_ref, out_ref, gathered, sems):
    count = gathered.shape[0]
    parts = sems.shape[0]
    size = count // parts
    copies = []
    for part in range(parts):
        def step(i, carry):
            k = part * size + i
            gathered[k] = held_ref[place_ref[k]]
            return carry

        lax.fori_loop(0, size, step, 0, unroll=32)
        run = pl.ds(part * size, size)
        copies.append(pltpu.make_async_copy(gathered.at[run], out_ref.at[run], sems.at[part]))
        copies[-1].start()
    for copy in copies:
        copy.wait()


def take(places, held):
    shape = places.shape + held.shape[1:]
    return pl.pallas_call(
        take_kernel,
        in_specs=[IN_SMEM, IN_VMEM],
        out_specs=ANYWHERE,
        out_shape=jax.ShapeDtypeStruct(shape, jnp.bfloat16),
        scratch_shapes=[pltpu.VMEM(shape, jnp.bfloat16), pltpu.SemaphoreType.DMA((2,))],
        compiler_params=pltpu.CompilerParams(vmem_limit_bytes=8 * MIB),
        cost_estimate=pl.CostEstimate(flops=0, bytes_accessed=2 * MIB, transcendentals=0),
    )(places, held)


def on_device(gradients, block_owners, left_stats, right_stats, left_roots, right_roots):
    rep_count = lax.axis_size("rep")
    owner_count = lax.axis_size("fsdp")
    slot_count = left_stats.shape[0]
    replica_rows = gradients[0]
    per_quarter = replica_rows.shape[0] // rep_count
    half = per_quarter // 2
    quarter = lax.axis_index("rep")

    def swap(value, bit):
        return lax.ppermute(value, "rep", [(i, i ^ bit) for i in range(rep_count)])

    def start(bit, second):
        return (quarter ^ bit) * per_quarter + second * half

    on_a = lax.dynamic_slice_in_dim(replica_rows, start(2, 0), half)
    on_b = lax.dynamic_slice_in_dim(replica_rows, start(2, 1), half)
    on_a, on_b = swap(on_a, 1), swap(on_b, 3)
    end_a, end_b = cut(replica_rows, [start(1, 0), start(3, 1)], [half] * 2)
    near_a, near_b = swap(end_a, 1), swap(end_b, 3)
    own, pass_a, pass_b = cut(
        replica_rows, [start(0, 0), start(3, 0), start(1, 1)], [per_quarter, half, half]
    )
    on_a, on_b = add(pass_a, on_a), add(pass_b, on_b)
    far_a, far_b = swap(on_a, 3), swap(on_b, 1)

    places = my_places(block_owners, quarter, per_quarter, slot_count)
    near = near_sum(own, near_a, near_b)
    placed = place(places, near, far_a, far_b, owner_count * slot_count)
    placed = placed.reshape((owner_count, slot_count) + placed.shape[1:])
    held = lax.all_to_all(placed, "fsdp", split_axis=0, concat_axis=0, tiled=True)
    update_slots = products(held, left_roots, right_roots)
    returned = lax.all_to_all(update_slots, "fsdp", split_axis=0, concat_axis=0, tiled=True)
    left_new, right_new = statistics(held, left_stats, right_stats)
    update = take(places, returned.reshape((-1,) + returned.shape[2:]))
    return (update, left_new, right_new)


def solution(mesh):
    placed = (
        P("rep", None, "fsdp", None),
        P(),
        P(("rep", "fsdp"), None, None),
        P(("rep", "fsdp"), None, None),
        P(("rep", "fsdp"), None, None),
        P(("rep", "fsdp"), None, None),
    )
    return jax.shard_map(
        on_device,
        mesh=mesh,
        in_specs=placed,
        out_specs=(
            P("rep", "fsdp", None),
            P(("rep", "fsdp"), None, None),
            P(("rep", "fsdp"), None, None),
        ),
        check_vma=False,
    )
```

```python
import jax
import jax.numpy as jnp
from jax import lax
from jax.experimental import pallas as pl
from jax.experimental.pallas import tpu as pltpu
from jax.sharding import PartitionSpec as P

MIB = 1024 * 1024
IN_VMEM = pl.BlockSpec(memory_space=pltpu.VMEM)
IN_SMEM = pl.BlockSpec(memory_space=pltpu.SMEM)
ANYWHERE = pl.BlockSpec(memory_space=pl.ANY)
IN_HBM = pl.BlockSpec(memory_space=pltpu.HBM)


def my_places(block_owners, quarter, per_quarter, slot_count):
    owners = lax.dynamic_slice(block_owners, (quarter * per_quarter, 0), (per_quarter, 1))
    same_owner = owners == owners.reshape(1, per_quarter)
    earlier = lax.broadcasted_iota(jnp.int32, (per_quarter, per_quarter), 1) < lax.broadcasted_iota(
        jnp.int32, (per_quarter, per_quarter), 0
    )
    rank = jnp.sum((same_owner & earlier).astype(jnp.int32), axis=1)
    return owners[:, 0] * slot_count + rank


def wide(value):
    return value.astype(jnp.float32)


def cut_kernel(starts_ref, rows_ref, *refs):
    outs, sems = refs[:-1], refs[-1]
    copies = []
    for i, out in enumerate(outs):
        copies.append(
            pltpu.make_async_copy(rows_ref.at[pl.ds(starts_ref[i], out.shape[0])], out, sems.at[i])
        )
    for copy in copies:
        copy.start()
    for copy in copies:
        copy.wait()


def cut(rows, starts, counts):
    return pl.pallas_call(
        cut_kernel,
        in_specs=[IN_SMEM, IN_HBM],
        out_specs=[IN_VMEM] * len(counts),
        out_shape=[pltpu.VMEM((count,) + rows.shape[1:], rows.dtype) for count in counts],
        scratch_shapes=[pltpu.SemaphoreType.DMA((len(counts),))],
        compiler_params=pltpu.CompilerParams(vmem_limit_bytes=8 * MIB),
        cost_estimate=pl.CostEstimate(flops=0, bytes_accessed=2 * MIB, transcendentals=0),
    )(jnp.stack(starts), pltpu.with_memory_space_constraint(rows, pltpu.HBM))


def add_kernel(a_ref, b_ref, sum_ref):
    sum_ref[...] = (wide(a_ref[...]) + wide(b_ref[...])).astype(jnp.bfloat16)


def add(a, b):
    return pl.pallas_call(
        add_kernel,
        in_specs=[IN_VMEM] * 2,
        out_specs=IN_VMEM,
        out_shape=jax.ShapeDtypeStruct(a.shape, a.dtype),
        compiler_params=pltpu.CompilerParams(vmem_limit_bytes=8 * MIB),
        cost_estimate=pl.CostEstimate(flops=a.size, bytes_accessed=MIB, transcendentals=0),
    )(a, b)


def near_kernel(own_ref, near_a_ref, near_b_ref, sum_ref, empty_ref):
    empty_ref[...] = jnp.zeros_like(empty_ref)
    half = near_a_ref.shape[0]
    sum_ref[:half] = wide(own_ref[:half]) + wide(near_a_ref[...])
    sum_ref[half:] = wide(own_ref[half:]) + wide(near_b_ref[...])


def near_sum(own, near_a, near_b, place_count):
    return pl.pallas_call(
        near_kernel,
        in_specs=[IN_VMEM] * 3,
        out_specs=[IN_VMEM] * 2,
        out_shape=[
            pltpu.VMEM(own.shape, jnp.float32),
            pltpu.VMEM((place_count,) + own.shape[1:], own.dtype),
        ],
        compiler_params=pltpu.CompilerParams(vmem_limit_bytes=8 * MIB),
        cost_estimate=pl.CostEstimate(flops=own.size, bytes_accessed=2 * MIB, transcendentals=0),
    )(own, near_a, near_b)


def place_kernel(place_ref, near_ref, far_a_ref, far_b_ref, empty_ref, out_ref):
    del empty_ref
    share = far_a_ref.shape[0]
    for first, far_ref in ((0, far_a_ref), (share, far_b_ref)):

        def step(i, carry, first=first, far_ref=far_ref):
            total = near_ref[first + i] + wide(far_ref[i])
            out_ref[place_ref[first + i]] = total.astype(jnp.bfloat16)
            return carry

        lax.fori_loop(0, share, step, 0, unroll=share)


def place(places, near, far_a, far_b, empty):
    return pl.pallas_call(
        place_kernel,
        in_specs=[IN_SMEM] + [IN_VMEM] * 4,
        out_specs=IN_VMEM,
        out_shape=jax.ShapeDtypeStruct(empty.shape, jnp.bfloat16),
        input_output_aliases={4: 0},
        compiler_params=pltpu.CompilerParams(vmem_limit_bytes=8 * MIB),
        cost_estimate=pl.CostEstimate(flops=near.size, bytes_accessed=3 * MIB, transcendentals=0),
    )(places, near, far_a, far_b, empty)


def product_kernel(held_ref, left_ref, right_ref, update_ref, made, sems):
    owner_count, slot_count, rows, order = held_ref.shape
    strips = sems.shape[1]
    height = order // strips
    copies = []
    for s in range(slot_count):
        block = wide(held_ref[:, s]).reshape(order, order).astype(jnp.bfloat16)
        half = jnp.dot(left_ref[s], block, preferred_element_type=jnp.float32).astype(jnp.bfloat16)
        for j in range(strips):
            full = jnp.dot(
                half[j * height : (j + 1) * height], right_ref[s], preferred_element_type=jnp.float32
            )
            run = pl.ds(j * height // rows, height // rows)
            made[s, run] = full.reshape(height // rows, rows, order).astype(jnp.bfloat16)
            copies.append(pltpu.make_async_copy(made.at[s, run], update_ref.at[run, s], sems.at[s, j]))
            copies[-1].start()
    for copy in copies:
        copy.wait()


def products(held, left_roots, right_roots):
    owner_count, slot_count, rows, order = held.shape
    return pl.pallas_call(
        product_kernel,
        in_specs=[IN_VMEM] * 3,
        out_specs=ANYWHERE,
        out_shape=jax.ShapeDtypeStruct(held.shape, jnp.bfloat16),
        scratch_shapes=[
            pltpu.VMEM((slot_count, owner_count, rows, order), jnp.bfloat16),
            pltpu.SemaphoreType.DMA((slot_count, 2)),
        ],
        compiler_params=pltpu.CompilerParams(vmem_limit_bytes=16 * MIB),
        cost_estimate=pl.CostEstimate(flops=2**30, bytes_accessed=4 * MIB, transcendentals=0),
    )(held, left_roots, right_roots)


def stats_kernel(held_ref, left_ref, right_ref, left_out, right_out):
    order = held_ref.shape[3]
    block = wide(held_ref[:, 0]).reshape(order, order).astype(jnp.bfloat16)
    left_out[0] = left_ref[0] + lax.dot_general(
        block, block, (((1,), (1,)), ((), ())), preferred_element_type=jnp.float32
    )
    right_out[0] = right_ref[0] + lax.dot_general(
        block, block, (((0,), (0,)), ((), ())), preferred_element_type=jnp.float32
    )


def statistics(held, left_stats, right_stats):
    owner_count, slot_count, rows, order = held.shape
    matrix = pl.BlockSpec((1, order, order), lambda s: (s, 0, 0))
    return pl.pallas_call(
        stats_kernel,
        grid=(slot_count,),
        in_specs=[pl.BlockSpec((owner_count, 1, rows, order), lambda s: (0, s, 0, 0)), matrix, matrix],
        out_specs=[matrix] * 2,
        out_shape=[jax.ShapeDtypeStruct(left_stats.shape, jnp.float32)] * 2,
        compiler_params=pltpu.CompilerParams(vmem_limit_bytes=24 * MIB),
        cost_estimate=pl.CostEstimate(flops=2**30, bytes_accessed=10 * MIB, transcendentals=0),
    )(held, left_stats, right_stats)


def take_kernel(place_ref, held_ref, out_ref, gathered, sems):
    count = gathered.shape[0]
    parts = sems.shape[0]
    size = count // parts
    copies = []
    for part in range(parts):
        def step(i, carry):
            k = part * size + i
            gathered[k] = held_ref[place_ref[k]]
            return carry

        lax.fori_loop(0, size, step, 0, unroll=32)
        run = pl.ds(part * size, size)
        copies.append(pltpu.make_async_copy(gathered.at[run], out_ref.at[run], sems.at[part]))
        copies[-1].start()
    for copy in copies:
        copy.wait()


def take(places, held):
    shape = places.shape + held.shape[1:]
    return pl.pallas_call(
        take_kernel,
        in_specs=[IN_SMEM, IN_VMEM],
        out_specs=ANYWHERE,
        out_shape=jax.ShapeDtypeStruct(shape, jnp.bfloat16),
        scratch_shapes=[pltpu.VMEM(shape, jnp.bfloat16), pltpu.SemaphoreType.DMA((2,))],
        compiler_params=pltpu.CompilerParams(vmem_limit_bytes=8 * MIB),
        cost_estimate=pl.CostEstimate(flops=0, bytes_accessed=2 * MIB, transcendentals=0),
    )(places, held)


def on_device(gradients, block_owners, left_stats, right_stats, left_roots, right_roots):
    rep_count = lax.axis_size("rep")
    owner_count = lax.axis_size("fsdp")
    slot_count = left_stats.shape[0]
    replica_rows = gradients[0]
    per_quarter = replica_rows.shape[0] // rep_count
    half = per_quarter // 2
    quarter = lax.axis_index("rep")

    def swap(value, bit):
        return lax.ppermute(value, "rep", [(i, i ^ bit) for i in range(rep_count)])

    def start(bit, second):
        return (quarter ^ bit) * per_quarter + second * half

    on_a = lax.dynamic_slice_in_dim(replica_rows, start(2, 0), half)
    on_b = lax.dynamic_slice_in_dim(replica_rows, start(2, 1), half)
    on_a, on_b = swap(on_a, 1), swap(on_b, 3)
    end_a, end_b = cut(replica_rows, [start(1, 0), start(3, 1)], [half] * 2)
    near_a, near_b = swap(end_a, 1), swap(end_b, 3)
    own, pass_a, pass_b = cut(
        replica_rows, [start(0, 0), start(3, 0), start(1, 1)], [per_quarter, half, half]
    )
    on_a, on_b = add(pass_a, on_a), add(pass_b, on_b)
    far_a, far_b = swap(on_a, 3), swap(on_b, 1)

    places = my_places(block_owners, quarter, per_quarter, slot_count)
    near, empty = near_sum(own, near_a, near_b, owner_count * slot_count)
    placed = place(places, near, far_a, far_b, empty)
    placed = placed.reshape((owner_count, slot_count) + placed.shape[1:])
    held = lax.all_to_all(placed, "fsdp", split_axis=0, concat_axis=0, tiled=True)
    update_slots = products(held, left_roots, right_roots)
    returned = lax.all_to_all(update_slots, "fsdp", split_axis=0, concat_axis=0, tiled=True)
    left_new, right_new = statistics(held, left_stats, right_stats)
    update = take(places, returned.reshape((-1,) + returned.shape[2:]))
    return (update, left_new, right_new)


def solution(mesh):
    placed = (
        P("rep", None, "fsdp", None),
        P(),
        P(("rep", "fsdp"), None, None),
        P(("rep", "fsdp"), None, None),
        P(("rep", "fsdp"), None, None),
        P(("rep", "fsdp"), None, None),
    )
    return jax.shard_map(
        on_device,
        mesh=mesh,
        in_specs=placed,
        out_specs=(
            P("rep", "fsdp", None),
            P(("rep", "fsdp"), None, None),
            P(("rep", "fsdp"), None, None),
        ),
        check_vma=False,
    )
```

```python
import jax
import jax.numpy as jnp
from jax import lax
from jax.experimental import pallas as pl
from jax.experimental.pallas import tpu as pltpu
from jax.sharding import PartitionSpec as P

MIB = 1024 * 1024
IN_VMEM = pl.BlockSpec(memory_space=pltpu.VMEM)
IN_SMEM = pl.BlockSpec(memory_space=pltpu.SMEM)
ANYWHERE = pl.BlockSpec(memory_space=pl.ANY)
IN_HBM = pl.BlockSpec(memory_space=pltpu.HBM)


def my_places(block_owners, quarter, per_quarter, slot_count):
    owners = lax.dynamic_slice(block_owners, (quarter * per_quarter, 0), (per_quarter, 1))
    same_owner = owners == owners.reshape(1, per_quarter)
    earlier = lax.broadcasted_iota(jnp.int32, (per_quarter, per_quarter), 1) < lax.broadcasted_iota(
        jnp.int32, (per_quarter, per_quarter), 0
    )
    rank = jnp.sum((same_owner & earlier).astype(jnp.int32), axis=1)
    return owners[:, 0] * slot_count + rank


def wide(value):
    return value.astype(jnp.float32)


def cut_kernel(starts_ref, rows_ref, *refs):
    outs, sems = refs[:-1], refs[-1]
    copies = []
    for i, out in enumerate(outs):
        copies.append(
            pltpu.make_async_copy(rows_ref.at[pl.ds(starts_ref[i], out.shape[0])], out, sems.at[i])
        )
    for copy in copies:
        copy.start()
    for copy in copies:
        copy.wait()


def cut(rows, starts, counts):
    return pl.pallas_call(
        cut_kernel,
        in_specs=[IN_SMEM, IN_HBM],
        out_specs=[IN_VMEM] * len(counts),
        out_shape=[pltpu.VMEM((count,) + rows.shape[1:], rows.dtype) for count in counts],
        scratch_shapes=[pltpu.SemaphoreType.DMA((len(counts),))],
        compiler_params=pltpu.CompilerParams(vmem_limit_bytes=8 * MIB),
        cost_estimate=pl.CostEstimate(flops=0, bytes_accessed=2 * MIB, transcendentals=0),
    )(jnp.stack(starts), pltpu.with_memory_space_constraint(rows, pltpu.HBM))


def add_kernel(a_ref, b_ref, sum_ref):
    sum_ref[...] = (wide(a_ref[...]) + wide(b_ref[...])).astype(jnp.bfloat16)


def add(a, b):
    return pl.pallas_call(
        add_kernel,
        in_specs=[IN_VMEM] * 2,
        out_specs=IN_VMEM,
        out_shape=jax.ShapeDtypeStruct(a.shape, a.dtype),
        compiler_params=pltpu.CompilerParams(vmem_limit_bytes=8 * MIB),
        cost_estimate=pl.CostEstimate(flops=a.size, bytes_accessed=MIB, transcendentals=0),
    )(a, b)


def near_kernel(own_ref, near_a_ref, near_b_ref, sum_ref, empty_ref):
    empty_ref[...] = jnp.zeros_like(empty_ref)
    half = near_a_ref.shape[0]
    sum_ref[:half] = wide(own_ref[:half]) + wide(near_a_ref[...])
    sum_ref[half:] = wide(own_ref[half:]) + wide(near_b_ref[...])


def near_sum(own, near_a, near_b, place_count):
    return pl.pallas_call(
        near_kernel,
        in_specs=[IN_VMEM] * 3,
        out_specs=[IN_VMEM] * 2,
        out_shape=[
            pltpu.VMEM(own.shape, jnp.float32),
            pltpu.VMEM((place_count,) + own.shape[1:], own.dtype),
        ],
        compiler_params=pltpu.CompilerParams(vmem_limit_bytes=8 * MIB),
        cost_estimate=pl.CostEstimate(flops=own.size, bytes_accessed=2 * MIB, transcendentals=0),
    )(own, near_a, near_b)


def place_kernel(place_ref, near_ref, far_a_ref, far_b_ref, empty_ref, out_ref):
    del empty_ref
    share = far_a_ref.shape[0]
    for first, far_ref in ((0, far_a_ref), (share, far_b_ref)):

        def step(i, carry, first=first, far_ref=far_ref):
            total = near_ref[first + i] + wide(far_ref[i])
            out_ref[place_ref[first + i]] = total.astype(jnp.bfloat16)
            return carry

        lax.fori_loop(0, share, step, 0, unroll=share)


def place(places, near, far_a, far_b, empty):
    return pl.pallas_call(
        place_kernel,
        in_specs=[IN_SMEM] + [IN_VMEM] * 4,
        out_specs=IN_VMEM,
        out_shape=jax.ShapeDtypeStruct(empty.shape, jnp.bfloat16),
        input_output_aliases={4: 0},
        compiler_params=pltpu.CompilerParams(vmem_limit_bytes=8 * MIB),
        cost_estimate=pl.CostEstimate(flops=near.size, bytes_accessed=3 * MIB, transcendentals=0),
    )(places, near, far_a, far_b, empty)


def product_kernel(held_ref, left_ref, right_ref, update_ref, made, sems):
    owner_count, slot_count, rows, order = held_ref.shape
    strips = sems.shape[1]
    height = order // strips
    copies = []
    for s in range(slot_count):
        block = wide(held_ref[:, s]).reshape(order, order).astype(jnp.bfloat16)
        half = jnp.dot(left_ref[s], block, preferred_element_type=jnp.float32).astype(jnp.bfloat16)
        for j in range(strips):
            full = jnp.dot(
                half[j * height : (j + 1) * height], right_ref[s], preferred_element_type=jnp.float32
            )
            run = pl.ds(j * height // rows, height // rows)
            made[s, run] = full.reshape(height // rows, rows, order).astype(jnp.bfloat16)
            copies.append(pltpu.make_async_copy(made.at[s, run], update_ref.at[run, s], sems.at[s, j]))
            copies[-1].start()
    for copy in copies:
        copy.wait()


def products(held, left_roots, right_roots):
    owner_count, slot_count, rows, order = held.shape
    return pl.pallas_call(
        product_kernel,
        in_specs=[IN_VMEM] * 3,
        out_specs=ANYWHERE,
        out_shape=jax.ShapeDtypeStruct(held.shape, jnp.bfloat16),
        scratch_shapes=[
            pltpu.VMEM((slot_count, owner_count, rows, order), jnp.bfloat16),
            pltpu.SemaphoreType.DMA((slot_count, 2)),
        ],
        compiler_params=pltpu.CompilerParams(vmem_limit_bytes=16 * MIB),
        cost_estimate=pl.CostEstimate(flops=2**30, bytes_accessed=4 * MIB, transcendentals=0),
    )(held, left_roots, right_roots)


def stats_kernel(held_ref, left_ref, right_ref, left_out, right_out):
    order = held_ref.shape[3]
    block = wide(held_ref[:, 0]).reshape(order, order).astype(jnp.bfloat16)
    left_out[0] = left_ref[0] + lax.dot_general(
        block, block, (((1,), (1,)), ((), ())), preferred_element_type=jnp.float32
    )
    right_out[0] = right_ref[0] + lax.dot_general(
        block, block, (((0,), (0,)), ((), ())), preferred_element_type=jnp.float32
    )


def statistics(held, left_stats, right_stats):
    owner_count, slot_count, rows, order = held.shape
    matrix = pl.BlockSpec((1, order, order), lambda s: (s, 0, 0))
    return pl.pallas_call(
        stats_kernel,
        grid=(slot_count,),
        in_specs=[pl.BlockSpec((owner_count, 1, rows, order), lambda s: (0, s, 0, 0)), matrix, matrix],
        out_specs=[matrix] * 2,
        out_shape=[jax.ShapeDtypeStruct(left_stats.shape, jnp.float32)] * 2,
        compiler_params=pltpu.CompilerParams(vmem_limit_bytes=24 * MIB),
        cost_estimate=pl.CostEstimate(flops=2**30, bytes_accessed=10 * MIB, transcendentals=0),
    )(
        held,
        pltpu.with_memory_space_constraint(left_stats, pltpu.HBM),
        pltpu.with_memory_space_constraint(right_stats, pltpu.HBM),
    )


def take_kernel(place_ref, held_ref, out_ref, gathered, sems):
    count = gathered.shape[0]
    parts = sems.shape[0]
    size = count // parts
    copies = []
    for part in range(parts):
        def step(i, carry):
            k = part * size + i
            gathered[k] = held_ref[place_ref[k]]
            return carry

        lax.fori_loop(0, size, step, 0, unroll=32)
        run = pl.ds(part * size, size)
        copies.append(pltpu.make_async_copy(gathered.at[run], out_ref.at[run], sems.at[part]))
        copies[-1].start()
    for copy in copies:
        copy.wait()


def take(places, held):
    shape = places.shape + held.shape[1:]
    return pl.pallas_call(
        take_kernel,
        in_specs=[IN_SMEM, IN_VMEM],
        out_specs=ANYWHERE,
        out_shape=jax.ShapeDtypeStruct(shape, jnp.bfloat16),
        scratch_shapes=[pltpu.VMEM(shape, jnp.bfloat16), pltpu.SemaphoreType.DMA((2,))],
        compiler_params=pltpu.CompilerParams(vmem_limit_bytes=8 * MIB),
        cost_estimate=pl.CostEstimate(flops=0, bytes_accessed=2 * MIB, transcendentals=0),
    )(places, held)


def on_device(gradients, block_owners, left_stats, right_stats, left_roots, right_roots):
    rep_count = lax.axis_size("rep")
    owner_count = lax.axis_size("fsdp")
    slot_count = left_stats.shape[0]
    replica_rows = gradients[0]
    per_quarter = replica_rows.shape[0] // rep_count
    half = per_quarter // 2
    quarter = lax.axis_index("rep")

    def swap(value, bit):
        return lax.ppermute(value, "rep", [(i, i ^ bit) for i in range(rep_count)])

    def start(bit, second):
        return (quarter ^ bit) * per_quarter + second * half

    on_a = lax.dynamic_slice_in_dim(replica_rows, start(2, 0), half)
    on_b = lax.dynamic_slice_in_dim(replica_rows, start(2, 1), half)
    on_a, on_b = swap(on_a, 1), swap(on_b, 3)
    end_a, end_b = cut(replica_rows, [start(1, 0), start(3, 1)], [half] * 2)
    near_a, near_b = swap(end_a, 1), swap(end_b, 3)
    own, pass_a, pass_b = cut(
        replica_rows, [start(0, 0), start(3, 0), start(1, 1)], [per_quarter, half, half]
    )
    on_a, on_b = add(pass_a, on_a), add(pass_b, on_b)
    far_a, far_b = swap(on_a, 3), swap(on_b, 1)

    places = my_places(block_owners, quarter, per_quarter, slot_count)
    near, empty = near_sum(own, near_a, near_b, owner_count * slot_count)
    placed = place(places, near, far_a, far_b, empty)
    placed = placed.reshape((owner_count, slot_count) + placed.shape[1:])
    held = lax.all_to_all(placed, "fsdp", split_axis=0, concat_axis=0, tiled=True)
    update_slots = products(held, left_roots, right_roots)
    returned = lax.all_to_all(update_slots, "fsdp", split_axis=0, concat_axis=0, tiled=True)
    left_new, right_new = statistics(held, left_stats, right_stats)
    update = take(places, returned.reshape((-1,) + returned.shape[2:]))
    return (update, left_new, right_new)


def solution(mesh):
    placed = (
        P("rep", None, "fsdp", None),
        P(),
        P(("rep", "fsdp"), None, None),
        P(("rep", "fsdp"), None, None),
        P(("rep", "fsdp"), None, None),
        P(("rep", "fsdp"), None, None),
    )
    return jax.shard_map(
        on_device,
        mesh=mesh,
        in_specs=placed,
        out_specs=(
            P("rep", "fsdp", None),
            P(("rep", "fsdp"), None, None),
            P(("rep", "fsdp"), None, None),
        ),
        check_vma=False,
    )
```

```python
import jax
import jax.numpy as jnp
from jax import lax
from jax.experimental import pallas as pl
from jax.experimental.pallas import tpu as pltpu
from jax.sharding import PartitionSpec as P

MIB = 1024 * 1024
IN_VMEM = pl.BlockSpec(memory_space=pltpu.VMEM)
IN_SMEM = pl.BlockSpec(memory_space=pltpu.SMEM)
ANYWHERE = pl.BlockSpec(memory_space=pl.ANY)
IN_HBM = pl.BlockSpec(memory_space=pltpu.HBM)


def my_places(block_owners, quarter, per_quarter, slot_count):
    owners = lax.dynamic_slice(block_owners, (quarter * per_quarter, 0), (per_quarter, 1))
    same_owner = owners == owners.reshape(1, per_quarter)
    earlier = lax.broadcasted_iota(jnp.int32, (per_quarter, per_quarter), 1) < lax.broadcasted_iota(
        jnp.int32, (per_quarter, per_quarter), 0
    )
    rank = jnp.sum((same_owner & earlier).astype(jnp.int32), axis=1)
    return owners[:, 0] * slot_count + rank


def wide(value):
    return value.astype(jnp.float32)


def cut_kernel(starts_ref, rows_ref, *refs):
    outs, sems = refs[:-1], refs[-1]
    copies = []
    for i, out in enumerate(outs):
        copies.append(
            pltpu.make_async_copy(rows_ref.at[pl.ds(starts_ref[i], out.shape[0])], out, sems.at[i])
        )
    for copy in copies:
        copy.start()
    for copy in copies:
        copy.wait()


def cut(rows, starts, counts):
    return pl.pallas_call(
        cut_kernel,
        in_specs=[IN_SMEM, IN_HBM],
        out_specs=[IN_VMEM] * len(counts),
        out_shape=[pltpu.VMEM((count,) + rows.shape[1:], rows.dtype) for count in counts],
        scratch_shapes=[pltpu.SemaphoreType.DMA((len(counts),))],
        compiler_params=pltpu.CompilerParams(vmem_limit_bytes=8 * MIB),
        cost_estimate=pl.CostEstimate(flops=0, bytes_accessed=2 * MIB, transcendentals=0),
    )(jnp.stack(starts), pltpu.with_memory_space_constraint(rows, pltpu.HBM))


def add_kernel(a_ref, b_ref, sum_ref):
    sum_ref[...] = (wide(a_ref[...]) + wide(b_ref[...])).astype(jnp.bfloat16)


def add(a, b):
    return pl.pallas_call(
        add_kernel,
        in_specs=[IN_VMEM] * 2,
        out_specs=IN_VMEM,
        out_shape=jax.ShapeDtypeStruct(a.shape, a.dtype),
        compiler_params=pltpu.CompilerParams(vmem_limit_bytes=8 * MIB),
        cost_estimate=pl.CostEstimate(flops=a.size, bytes_accessed=MIB, transcendentals=0),
    )(a, b)


def near_kernel(own_ref, near_a_ref, near_b_ref, sum_ref, empty_ref):
    empty_ref[...] = jnp.zeros_like(empty_ref)
    half = near_a_ref.shape[0]
    sum_ref[:half] = wide(own_ref[:half]) + wide(near_a_ref[...])
    sum_ref[half:] = wide(own_ref[half:]) + wide(near_b_ref[...])


def near_sum(own, near_a, near_b, place_count):
    return pl.pallas_call(
        near_kernel,
        in_specs=[IN_VMEM] * 3,
        out_specs=[IN_VMEM] * 2,
        out_shape=[
            pltpu.VMEM(own.shape, jnp.float32),
            pltpu.VMEM((place_count,) + own.shape[1:], own.dtype),
        ],
        compiler_params=pltpu.CompilerParams(vmem_limit_bytes=8 * MIB),
        cost_estimate=pl.CostEstimate(flops=own.size, bytes_accessed=2 * MIB, transcendentals=0),
    )(own, near_a, near_b)


def place_kernel(place_ref, near_ref, far_a_ref, far_b_ref, empty_ref, out_ref):
    del empty_ref
    share = far_a_ref.shape[0]
    for first, far_ref in ((0, far_a_ref), (share, far_b_ref)):

        def step(i, carry, first=first, far_ref=far_ref):
            total = near_ref[first + i] + wide(far_ref[i])
            out_ref[place_ref[first + i]] = total.astype(jnp.bfloat16)
            return carry

        lax.fori_loop(0, share, step, 0, unroll=share)


def place(places, near, far_a, far_b, empty):
    return pl.pallas_call(
        place_kernel,
        in_specs=[IN_SMEM] + [IN_VMEM] * 4,
        out_specs=IN_VMEM,
        out_shape=jax.ShapeDtypeStruct(empty.shape, jnp.bfloat16),
        input_output_aliases={4: 0},
        compiler_params=pltpu.CompilerParams(vmem_limit_bytes=8 * MIB),
        cost_estimate=pl.CostEstimate(flops=near.size, bytes_accessed=3 * MIB, transcendentals=0),
    )(places, near, far_a, far_b, empty)


def product_kernel(held_ref, left_ref, right_ref, update_ref, made, sems):
    owner_count, slot_count, rows, order = held_ref.shape
    strips = sems.shape[1]
    height = order // strips
    copies = []
    halves = []
    for s in range(slot_count):
        block = wide(held_ref[:, s]).reshape(order, order).astype(jnp.bfloat16)
        halves.append(
            jnp.dot(left_ref[s], block, preferred_element_type=jnp.float32).astype(jnp.bfloat16)
        )
    for s in range(slot_count):
        for j in range(strips):
            full = jnp.dot(
                halves[s][j * height : (j + 1) * height], right_ref[s], preferred_element_type=jnp.float32
            )
            run = pl.ds(j * height // rows, height // rows)
            made[s, run] = full.reshape(height // rows, rows, order).astype(jnp.bfloat16)
            copies.append(pltpu.make_async_copy(made.at[s, run], update_ref.at[run, s], sems.at[s, j]))
            copies[-1].start()
    for copy in copies:
        copy.wait()


def products(held, left_roots, right_roots):
    owner_count, slot_count, rows, order = held.shape
    return pl.pallas_call(
        product_kernel,
        in_specs=[IN_VMEM] * 3,
        out_specs=ANYWHERE,
        out_shape=jax.ShapeDtypeStruct(held.shape, jnp.bfloat16),
        scratch_shapes=[
            pltpu.VMEM((slot_count, owner_count, rows, order), jnp.bfloat16),
            pltpu.SemaphoreType.DMA((slot_count, 2)),
        ],
        compiler_params=pltpu.CompilerParams(vmem_limit_bytes=16 * MIB),
        cost_estimate=pl.CostEstimate(flops=2**30, bytes_accessed=4 * MIB, transcendentals=0),
    )(held, left_roots, right_roots)


def stats_kernel(held_ref, left_ref, right_ref, left_out, right_out):
    order = held_ref.shape[3]
    block = wide(held_ref[:, 0]).reshape(order, order).astype(jnp.bfloat16)
    left_out[0] = left_ref[0] + lax.dot_general(
        block, block, (((1,), (1,)), ((), ())), preferred_element_type=jnp.float32
    )
    right_out[0] = right_ref[0] + lax.dot_general(
        block, block, (((0,), (0,)), ((), ())), preferred_element_type=jnp.float32
    )


def statistics(held, left_stats, right_stats):
    owner_count, slot_count, rows, order = held.shape
    matrix = pl.BlockSpec((1, order, order), lambda s: (s, 0, 0))
    return pl.pallas_call(
        stats_kernel,
        grid=(slot_count,),
        in_specs=[pl.BlockSpec((owner_count, 1, rows, order), lambda s: (0, s, 0, 0)), matrix, matrix],
        out_specs=[matrix] * 2,
        out_shape=[jax.ShapeDtypeStruct(left_stats.shape, jnp.float32)] * 2,
        compiler_params=pltpu.CompilerParams(vmem_limit_bytes=24 * MIB),
        cost_estimate=pl.CostEstimate(flops=2**30, bytes_accessed=10 * MIB, transcendentals=0),
    )(
        held,
        pltpu.with_memory_space_constraint(left_stats, pltpu.HBM),
        pltpu.with_memory_space_constraint(right_stats, pltpu.HBM),
    )


def take_kernel(place_ref, held_ref, out_ref, gathered, sems):
    count = gathered.shape[0]
    parts = sems.shape[0]
    size = count // parts
    copies = []
    for part in range(parts):
        def step(i, carry):
            k = part * size + i
            gathered[k] = held_ref[place_ref[k]]
            return carry

        lax.fori_loop(0, size, step, 0, unroll=32)
        run = pl.ds(part * size, size)
        copies.append(pltpu.make_async_copy(gathered.at[run], out_ref.at[run], sems.at[part]))
        copies[-1].start()
    for copy in copies:
        copy.wait()


def take(places, held):
    shape = places.shape + held.shape[1:]
    return pl.pallas_call(
        take_kernel,
        in_specs=[IN_SMEM, IN_VMEM],
        out_specs=ANYWHERE,
        out_shape=jax.ShapeDtypeStruct(shape, jnp.bfloat16),
        scratch_shapes=[pltpu.VMEM(shape, jnp.bfloat16), pltpu.SemaphoreType.DMA((2,))],
        compiler_params=pltpu.CompilerParams(vmem_limit_bytes=8 * MIB),
        cost_estimate=pl.CostEstimate(flops=0, bytes_accessed=2 * MIB, transcendentals=0),
    )(places, held)


def on_device(gradients, block_owners, left_stats, right_stats, left_roots, right_roots):
    rep_count = lax.axis_size("rep")
    owner_count = lax.axis_size("fsdp")
    slot_count = left_stats.shape[0]
    replica_rows = gradients[0]
    per_quarter = replica_rows.shape[0] // rep_count
    half = per_quarter // 2
    quarter = lax.axis_index("rep")

    def swap(value, bit):
        return lax.ppermute(value, "rep", [(i, i ^ bit) for i in range(rep_count)])

    def start(bit, second):
        return (quarter ^ bit) * per_quarter + second * half

    on_a = lax.dynamic_slice_in_dim(replica_rows, start(2, 0), half)
    on_b = lax.dynamic_slice_in_dim(replica_rows, start(2, 1), half)
    on_a, on_b = swap(on_a, 1), swap(on_b, 3)
    end_a, end_b = cut(replica_rows, [start(1, 0), start(3, 1)], [half] * 2)
    near_a, near_b = swap(end_a, 1), swap(end_b, 3)
    own, pass_a, pass_b = cut(
        replica_rows, [start(0, 0), start(3, 0), start(1, 1)], [per_quarter, half, half]
    )
    on_a, on_b = add(pass_a, on_a), add(pass_b, on_b)
    far_a, far_b = swap(on_a, 3), swap(on_b, 1)

    places = my_places(block_owners, quarter, per_quarter, slot_count)
    near, empty = near_sum(own, near_a, near_b, owner_count * slot_count)
    placed = place(places, near, far_a, far_b, empty)
    placed = placed.reshape((owner_count, slot_count) + placed.shape[1:])
    held = lax.all_to_all(placed, "fsdp", split_axis=0, concat_axis=0, tiled=True)
    update_slots = products(held, left_roots, right_roots)
    returned = lax.all_to_all(update_slots, "fsdp", split_axis=0, concat_axis=0, tiled=True)
    left_new, right_new = statistics(held, left_stats, right_stats)
    update = take(places, returned.reshape((-1,) + returned.shape[2:]))
    return (update, left_new, right_new)


def solution(mesh):
    placed = (
        P("rep", None, "fsdp", None),
        P(),
        P(("rep", "fsdp"), None, None),
        P(("rep", "fsdp"), None, None),
        P(("rep", "fsdp"), None, None),
        P(("rep", "fsdp"), None, None),
    )
    return jax.shard_map(
        on_device,
        mesh=mesh,
        in_specs=placed,
        out_specs=(
            P("rep", "fsdp", None),
            P(("rep", "fsdp"), None, None),
            P(("rep", "fsdp"), None, None),
        ),
        check_vma=False,
    )
```
